32 devices in a mesh: dp: 8 (over y, x, core), tensor: 4 (over z).
Axes of the slice: x: 2, y: 2, z: 4, core: 2. Of those that a mesh axis runs over, the one named last changes fastest.
Arguments:
- inputs: bfloat16 [4096, 5120], P(('dp', 'tensor')), may hold values from -6 to 6
- latent: bfloat16 [4096, 512], P(('dp', 'tensor')), may hold values from -180 to 180
- gain: float32 [512], replicated, may hold values from 0.25 to 1.75
- w_latent: bfloat16 [5120, 512], P('tensor'), may hold values from -0.078125 to 0.078125
- w_rope: bfloat16 [5120, 64], P('tensor'), may hold values from -0.078125 to 0.078125
- w_up: bfloat16 [512, 32768], P('dp', 'tensor'), may hold values from -0.25 to 0.25
- grad_kv: bfloat16 [4096, 32768], P('dp', 'tensor'), may hold values from -6 to 6
- grad_rope: bfloat16 [4096, 64], P(('dp', 'tensor')), may hold values from -6 to 6
Outputs:
- grad_x: bfloat16 [4096, 5120], P(('dp', 'tensor'))
- grad_w_up: bfloat16 [512, 32768], P('dp', 'tensor')
- grad_w_latent: bfloat16 [5120, 512], P('tensor', 'dp')
- grad_w_rope: bfloat16 [5120, 64], P('tensor', 'dp')
- grad_gain: float32 [512], replicated
The draws below stay inside these ranges and needn't reach their ends.
All inputs are finite; a program needn't handle non-finite values.
Results may differ from the reference program's by a relative error of at most 0.019.
Values may be sent and summed in bfloat16 or wider, within the bound.
No kernel may reach another device: no remote copies, remote signals or barrier semaphores. Data moves between devices by JAX's collectives and lax.ppermute only.
A program may use at most 128 MiB of HBM per device.

```python
import math
import jax
import jax.numpy as jnp
from jax import lax

D = 5120
LAT = 512
ROPE = 64
HEADS = 128
HDIM = 128
VDIM = 128
TOKENS = 4096


def draw_latent(key, part):
    key = jax.random.fold_in(key, 7)
    key_base, key_rows, key_cols = jax.random.split(key, 3)
    row_scale = jnp.exp(jax.random.uniform(key_rows, (TOKENS, 1), minval=0.0, maxval=math.log(10.0)))
    col_scale = jnp.exp(jax.random.uniform(key_cols, (1, LAT), minval=0.0, maxval=math.log(10.0)))
    base_values = jax.random.normal(key_base, (TOKENS, LAT))
    base_values = jnp.clip(base_values, -6.0, 6.0)
    return (base_values * row_scale * col_scale * 0.3).astype(jnp.bfloat16)


def block_scale(own_key, shape, cuts, least, largest):
    loudness = 1.0
    for axis_at, shards_of in cuts:
        draws = jax.random.uniform(jax.random.fold_in(jax.random.fold_in(own_key, 6), axis_at), (shards_of,), jnp.float32, least / len(cuts), largest / len(cuts))
        loudness = loudness * jnp.repeat(jnp.exp(draws), shape[axis_at] // shards_of).reshape((-1,) + (1,) * (len(shape) - 1 - axis_at))
    return loudness


def centred(key, dims, width, limit, cuts=(), held_as=jnp.bfloat16):
    result = jax.random.normal(key, dims, jnp.float32) * width
    if len(cuts) > 0:
        result = block_scale(key, dims, cuts, -0.22, 0.18) * result
    return jnp.clip(result, min=-limit, max=limit).astype(held_as)


def setup_inputs(seed: int = 0) -> dict:
    key_of = jax.random.split(jax.random.key(seed), 9)
    inputs = centred(key_of[0], (TOKENS, D), 1.0, 6.0, ((0, 32),))
    latent = draw_latent(jax.random.fold_in(key_of[8], 71), 0)
    gain = jnp.clip(1.0 + 0.15 * jax.random.normal(key_of[2], (LAT,), jnp.float32), 0.25, 1.75)
    w_latent = centred(key_of[3], (D, LAT), D ** -0.5, 0.078125, ((0, 4),))
    w_rope = centred(key_of[4], (D, ROPE), D ** -0.5, 0.078125, ((0, 4),))
    w_up = centred(key_of[5], (LAT, HEADS * (HDIM + VDIM)), LAT ** -0.5, 0.25, ((0, 8), (1, 4)))
    grad_kv = centred(key_of[6], (TOKENS, HEADS * (HDIM + VDIM)), 1.0, 6.0, ((0, 8), (1, 4)))
    grad_rope = centred(key_of[7], (TOKENS, ROPE), 1.0, 6.0, ((0, 32),))
    return {"inputs": inputs, "latent": latent, "gain": gain, "w_latent": w_latent, "w_rope": w_rope, "w_up": w_up, "grad_kv": grad_kv, "grad_rope": grad_rope}


epsilon = 1e-06

def reference(inputs, latent, gain, w_latent, w_rope, w_up, grad_kv, grad_rope):
    latent_f = latent.astype(jnp.float32)
    inverse = lax.rsqrt(lax.optimization_barrier(jnp.mean(latent_f * latent_f, axis=-1, keepdims=True)) + epsilon)
    normed = (latent_f * inverse * gain).astype(jnp.bfloat16)
    grad_w_up = jnp.dot(normed.T, grad_kv, preferred_element_type=jnp.float32).astype(jnp.bfloat16)
    grad_norm = jnp.dot(grad_kv, w_up.T, preferred_element_type=jnp.float32)
    grad_gain = lax.optimization_barrier(jnp.sum(grad_norm * latent_f * inverse, axis=0))
    scaled = grad_norm * gain
    grad_pre = inverse * scaled - latent_f * inverse ** 3 * lax.optimization_barrier(jnp.mean(scaled * latent_f, axis=-1, keepdims=True))
    grad_pre = grad_pre.astype(jnp.bfloat16)
    grad_x = jnp.dot(grad_pre, w_latent.T, preferred_element_type=jnp.float32) + jnp.dot(grad_rope, w_rope.T, preferred_element_type=jnp.float32)
    grad_w_latent = jnp.dot(inputs.T, grad_pre, preferred_element_type=jnp.float32)
    grad_w_rope = jnp.dot(inputs.T, grad_rope, preferred_element_type=jnp.float32)
    return (grad_x.astype(jnp.bfloat16), grad_w_up, grad_w_latent.astype(jnp.bfloat16), grad_w_rope.astype(jnp.bfloat16), grad_gain)
```

```python
import functools

import jax
import jax.numpy as jnp
import numpy as np
from jax import lax
from jax.experimental import pallas as pl
from jax.experimental.pallas import tpu as pltpu
from jax.sharding import PartitionSpec as P

epsilon = 1e-06
W_U, W_M1, W_M2, W_COL, W_LAT = 2, 0, 16, 1, 8
LIMIT_U, LIMIT_M = 12, 12
F32 = jnp.float32
BF16 = jnp.bfloat16
VMEM = pl.BlockSpec(memory_space=pltpu.VMEM)
SMEM = pl.BlockSpec(memory_space=pltpu.SMEM)
GAIN_ROWS = 16


def dot(left, right, left_dim, right_dim):
    return lax.dot_general(
        left, right, (((left_dim,), (right_dim,)), ((), ())), preferred_element_type=F32
    )


def popcount(value):
    return bin(value).count("1")


def after(x, *done):
    return lax.optimization_barrier((x,) + done)[0]


def work(flops, moved, weight):
    return pl.CostEstimate(flops=weight * flops, bytes_accessed=weight * moved, transcendentals=0)


def call(body, name, out_shape, flops, weight, *args, scratch=(), limit=16):
    moved = sum(a.size * a.dtype.itemsize for a in args)
    return pl.pallas_call(
        body,
        in_specs=[SMEM] + [VMEM] * (len(args) - 1),
        out_specs=jax.tree.map(lambda _: VMEM, out_shape),
        out_shape=out_shape,
        scratch_shapes=scratch,
        compiler_params=pltpu.CompilerParams(vmem_limit_bytes=limit * 2**20),
        cost_estimate=work(flops, moved, weight),
        name=name,
    )(*args)


def split_rows(x, count, rows):
    at = lax.broadcasted_iota(jnp.int32, (rows, x.shape[1]), 0)
    result = jnp.zeros((rows, x.shape[1]), F32)
    for i in range(count):
        part = x.astype(BF16).astype(F32)
        result = jnp.where(at == i, part, result)
        x = x - part
    return result.astype(BF16)


class Plan:
    def __init__(self, groups, lanes, lat, rope):
        self.groups, self.lanes, self.lat, self.rope = groups, lanes, lat, rope
        self.axes = groups.bit_length() - 2
        self.slots = sorted(range(groups // 2), key=lambda slot: (popcount(slot), slot))
        middle = len(self.slots) // 2
        self.near, self.last = self.slots[:middle], self.slots[middle:]
        self.blk, self.rblk = lat // groups, rope // groups
        self.rb = max(self.rblk, 8)
        self.order = [(core, slot) for part in (self.near, self.last)
                      for core in (0, 1) for slot in part]

    def across(self, slot, core):
        bits = [self.axes - 1 - i if core else i for i in range(self.axes) if slot >> i & 1]
        return sum(2 << bit for bit in bits)

    def hop(self, slot):
        return 1 << (slot.bit_length() - 1)

    def rows_of(self, core):
        part = len(self.near) * self.blk
        first, second = core * part, (2 + core) * part
        return (first, first + part), (second, second + part)

    def pick_core(self, x, core):
        return jnp.concatenate([x[a:b] for a, b in self.rows_of(core)], axis=0)

    def place(self, me, order, block, stride):
        size, count = len(order) * stride, self.groups * block
        row = lax.broadcasted_iota(jnp.int32, (size, 1), 0)
        spot = jnp.full((size, 1), -1, jnp.int32)
        for b, (core, slot) in enumerate(order):
            rel = jnp.where(me % 2 == 0, self.across(slot, core) + core, self.across(slot, 1 - core) + core)
            start = (me ^ rel) * block
            inside = (row >= b * stride) & (row < b * stride + block)
            spot = jnp.where(inside, start + (row - b * stride), spot)
        column = lax.broadcasted_iota(jnp.int32, (size, count), 1)
        return (column == spot).astype(F32).astype(BF16)

    def place_latent(self, me):
        return self.place(me, self.order, self.blk, self.blk)

    def place_rope(self, me):
        order = [(core, slot) for core in (0, 1) for slot in self.slots]
        return self.place(me, order, self.rblk, self.rb)


def prep_kernel(plan, ids, gain, *refs):
    pieces, out_ref = refs[:-1], refs[-1]
    me, lane = ids[0], ids[1]
    tokens = pieces[0].shape[0]
    place = plan.place_latent(me)
    gain_col = jnp.sum(dot(place, split_rows(gain[...], 3, 8), 1, 1), axis=1, keepdims=True)
    for k, piece in enumerate(pieces):
        x = dot(place, piece[...], 1, 1)
        inverse = lax.rsqrt(jnp.sum(x * x, axis=0, keepdims=True) / plan.lat + epsilon)
        normed = (x * inverse * gain_col).astype(BF16)
        normed = jnp.concatenate([plan.pick_core(normed, 1), plan.pick_core(normed, 0)], axis=0)
        start = pl.multiple_of(lax.rem(lane - k + plan.lanes, plan.lanes) * tokens, tokens)
        out_ref[:, pl.ds(start, tokens)] = normed


def load_kernel(ids, x_ref, out_ref, sems):
    rows = x_ref.shape[0] // sems.shape[0]
    copies = [pltpu.make_async_copy(x_ref.at[pl.ds(i * rows, rows)], out_ref.at[pl.ds(i * rows, rows)],
                                    sems.at[i]) for i in range(sems.shape[0])]
    for copy in copies:
        copy.start()
    for copy in copies:
        copy.wait()


def load(ids, x):
    return pl.pallas_call(
        load_kernel,
        in_specs=[SMEM, pl.BlockSpec(memory_space=pltpu.HBM)],
        out_specs=VMEM,
        out_shape=pltpu.VMEM(x.shape, x.dtype),
        scratch_shapes=[pltpu.SemaphoreType.DMA((8,))],
        compiler_params=pltpu.CompilerParams(vmem_limit_bytes=2 * 2**20),
        cost_estimate=work(0, 0, 0),
        name="load",
    )(ids, x)


def up_kernel(ids, normed_ref, kv_ref, theirs_ref, *mine):
    half = theirs_ref.shape[0]
    rows = half // len(mine)
    depth = kv_ref.shape[1]
    step = min(depth, 1024)

    @pl.loop(0, depth // step)
    def _(k):
        at = pl.ds(pl.multiple_of(k * step, step), step)
        part = jnp.dot(normed_ref[...], kv_ref[:, at], preferred_element_type=F32)
        theirs_ref[:, at] = part[:half].astype(BF16)
        for i, out_ref in enumerate(mine):
            out_ref[:, at] = part[half + i * rows:half + (i + 1) * rows].astype(BF16)


def up_product(ids, normed_t, kv, count, weight):
    size, tokens = normed_t.shape
    depth = kv.shape[1]
    half = size // 2
    shapes = [half] + [half // count] * count
    return call(up_kernel, "up_product", [shape(rows, depth) for rows in shapes],
                2 * size * tokens * depth, weight, ids, normed_t, kv, limit=LIMIT_U)


def heads_kernel(count, lanes, ids, kv_ref, *refs):
    rows, before, outs, total = refs[:count], refs[count:-lanes - 1], refs[-lanes - 1:-1], refs[-1]
    depth = kv_ref.shape[1]
    step = min(depth, 1024)
    total[...] = jnp.zeros_like(total)

    @pl.loop(0, depth // step)
    def _(k):
        at = pl.ds(pl.multiple_of(k * step, step), step)
        total[...] += dot(kv_ref[:, at], jnp.concatenate([r[:, at] for r in rows], axis=0), 1, 1)

    tokens, columns = outs[0].shape[0], total.shape[1]
    for k, out_ref in enumerate(outs):
        start = pl.multiple_of(lax.rem(ids[1] + k, lanes) * tokens, tokens)
        if before:
            out_ref[:, :columns] = before[k][...]
        out_ref[:, out_ref.shape[1] - columns:] = total[pl.ds(start, tokens), :].astype(BF16)


def heads_product(ids, kv, rows, before, lanes, weight):
    tokens, depth = kv.shape
    width = sum(r.shape[0] for r in rows)
    out = shape(tokens // lanes, width + sum(b.shape[1] for b in before[:1]))
    return call(functools.partial(heads_kernel, len(rows), lanes), "heads_product", [out] * lanes,
                2 * tokens * depth * width, weight, ids, kv, *rows, *before,
                scratch=[pltpu.VMEM((tokens, width), F32)], limit=LIMIT_M)


def pre_kernel(plan, ids, latent, gain, rope_t, *refs):
    lanes = plan.lanes
    heads, out_ref = refs[:lanes], refs[lanes]
    tokens = latent.shape[0]
    place = plan.place_latent(ids[0])
    x = dot(latent[...], place, 1, 1)
    gain_row = jnp.sum(dot(split_rows(gain[...], 3, 8), place, 1, 1), axis=0, keepdims=True)
    grad_norm = sum(r[...].astype(F32) for r in heads)
    inverse = lax.rsqrt(jnp.sum(x * x, axis=1, keepdims=True) / plan.lat + epsilon)
    scaled = grad_norm * gain_row
    mean = jnp.sum(scaled * x, axis=1, keepdims=True) / plan.lat
    pre = inverse * scaled - x * (inverse * inverse * inverse) * mean
    out_ref[:tokens] = pre.astype(BF16)
    part = jnp.sum(grad_norm * x * inverse, axis=0, keepdims=True)
    part = jnp.sum(dot(split_rows(part, 3, 8), place, 1, 0), axis=0, keepdims=True)
    out_ref[tokens:tokens + GAIN_ROWS] = split_rows(part, 2, GAIN_ROWS)
    blocks = plan.lat // tokens
    rows = plan.rope // blocks
    out_ref[tokens + GAIN_ROWS:] = jnp.concatenate(
        [rope_t[i * rows:(i + 1) * rows, :] for i in range(blocks)], axis=1)


def rope_of(plan, message, tokens):
    blocks = plan.lat // tokens
    packed = message[tokens + GAIN_ROWS:]
    return jnp.concatenate(
        [packed[:, i * tokens:(i + 1) * tokens] for i in range(blocks)], axis=0)


def columns_kernel(plan, tokens, ids, *refs):
    lanes = plan.lanes
    messages, w_latent, w_rope_t, outs = refs[:lanes], refs[lanes], refs[lanes + 1], refs[lanes + 2:]
    pre = jnp.concatenate([m[:tokens] for m in messages], axis=0)
    pre = dot(pre, plan.place_latent(ids[0]), 1, 0).astype(BF16)
    rope = jnp.concatenate([rope_of(plan, m, tokens) for m in messages], axis=1)
    result = (dot(pre, w_latent[...], 1, 1) + dot(rope, w_rope_t[...], 0, 0)).astype(BF16)
    for k, out_ref in enumerate(outs):
        out_ref[...] = result[k * tokens:(k + 1) * tokens]


def gain_block(x, width):
    both = split_rows(x, 2, 8).astype(F32)
    row = jnp.concatenate([both[0:1], both[1:2]], axis=1)
    cut = row.shape[1]
    while cut > width:
        cut //= 2
    at = lax.broadcasted_iota(jnp.int32, (8, cut), 0)
    result = jnp.zeros((8, cut), F32)
    for i in range(row.shape[1] // cut):
        result = jnp.where(at == i, row[:, i * cut:(i + 1) * cut], result)
    if cut < width:
        result = jnp.concatenate([result, jnp.zeros((8, width - cut), F32)], axis=1)
    return result


def gain_of(block, lat):
    cut = 2 * lat
    while cut > block.shape[1]:
        cut //= 2
    row = jnp.concatenate([block[i:i + 1, :cut] for i in range(2 * lat // cut)], axis=1)
    return row[:, :lat] + row[:, lat:]


def latent_kernel(plan, tokens, ids, *refs):
    lanes = plan.lanes
    messages, spread, other_ref, own_ref = refs[:lanes], refs[lanes:2 * lanes], refs[-2], refs[-1]
    lane = ids[1]
    width = spread[0].shape[1]
    far = [lax.rem(lane - k + lanes, lanes) for k in range(lanes)]
    spread = jnp.concatenate([r[...] for r in spread], axis=0)
    pre = jnp.concatenate([m[:tokens] for m in messages], axis=0)
    rope_t = jnp.concatenate([rope_of(plan, m, tokens) for m in messages], axis=1)
    rope_t = dot(plan.place_rope(ids[0]), rope_t, 1, 0).astype(BF16)
    lat_rows = dot(pre, spread, 0, 0)
    rope_rows = dot(rope_t, spread, 1, 0)
    parts = [jnp.sum(m[tokens:tokens + GAIN_ROWS].astype(F32), axis=0, keepdims=True)
             for m in messages]
    total = jnp.zeros_like(parts[0])
    for j in range(lanes):
        term = parts[0]
        for k in range(1, lanes):
            term = jnp.where(far[j] == k, parts[k], term)
        total = total + term
    gain = gain_block(total, width)
    n = len(plan.slots) * plan.rb
    for core, ref in ((1, other_ref), (0, own_ref)):
        rows = jnp.concatenate(
            [plan.pick_core(lat_rows, core), rope_rows[core * n:(core + 1) * n],
             gain, jnp.zeros_like(gain)], axis=0)
        ref[...] = rows.astype(ref.dtype)


def chip_kernel(plan, ids, own, other, *outs):
    half, n = plan.lat // 2, len(plan.slots) * plan.rb
    width = own.shape[1]
    mine, came = own[...], other[...].astype(F32)
    total = mine + came
    gain = gain_of(mine[half + n:half + n + 8], plan.lat) + gain_of(came[half + n:half + n + 8], plan.lat)
    gain = gain_block(gain, width)
    for i, out_ref in enumerate(outs):
        rows = jnp.concatenate(
            [total[i * plan.blk:(i + 1) * plan.blk],
             total[half + i * plan.rb:half + (i + 1) * plan.rb], gain], axis=0)
        out_ref[...] = rows.astype(out_ref.dtype)


def last_kernel(plan, ids, *refs):
    count = len(plan.slots)
    back, sums = refs[:plan.lanes], refs[plan.lanes:plan.lanes + count]
    lat_ref, rope_ref, gain_ref, x_ref = refs[plan.lanes + count:]
    width = back[0].shape[1]
    for k, piece in enumerate(back):
        if width % 128 == 0:
            start = pl.multiple_of(lax.rem(ids[1] + k, plan.lanes) * width, width)
        else:
            start = k * width
        x_ref[:, pl.ds(start, width)] = piece[...]
    blk, rb = plan.blk, plan.rb
    me = ids[0]
    sums = [r[...].astype(F32) for r in sums]
    total = sum(s[:blk + rb] for s in sums)
    lat_ref[...] = total[:blk].astype(BF16)
    rope_ref[...] = total[blk:blk + rb].astype(BF16)
    parts = [gain_of(s[blk + rb:blk + rb + 8], plan.lat) for s in sums]
    gain = jnp.zeros_like(parts[0])
    for chip in range(plan.groups // 2):
        term = jnp.zeros_like(parts[0])
        for slot, part in zip(plan.slots, parts):
            rel = jnp.where(me % 2 == 0, plan.across(slot, 0) // 2, plan.across(slot, 1) // 2)
            term = jnp.where((rel ^ (me // 2)) == chip, part, term)
        gain = gain + term
    gain_ref[...] = gain


def cut_kernel(lanes, ids, x, *outs):
    width = outs[0].shape[1]
    for k, out_ref in enumerate(outs):
        start = pl.multiple_of(lax.rem(ids[1] + k, lanes) * width, width)
        out_ref[...] = x[:, pl.ds(start, width)]


def pick(pieces, index):
    result = pieces[0]
    for i in range(1, len(pieces)):
        result = jnp.where(index == i, pieces[i], result)
    return result


def add_kernel(*refs):
    refs[-1][...] = sum(r[...].astype(F32) for r in refs[:-1]).astype(BF16)


def add(*parts):
    parts = [p if isinstance(p, tuple) else (p, 0) for p in parts]
    rows, depth = parts[0][0].shape
    step = min(depth, 2048)
    return pl.pallas_call(
        add_kernel,
        grid=(depth // step,),
        in_specs=[pl.BlockSpec((rows, step), lambda k, at=at: (at // rows, k)) for _, at in parts],
        out_specs=pl.BlockSpec((rows, step), lambda k: (0, k)),
        out_shape=shape(rows, depth),
        compiler_params=pltpu.CompilerParams(vmem_limit_bytes=8 * 2**20),
        cost_estimate=work(0, 2 * rows * depth * (len(parts) + 1), 1),
        name="add",
    )(*[p for p, _ in parts])


def shape(rows, columns, dtype=BF16):
    return jax.ShapeDtypeStruct((rows, columns), dtype)


def make_shards(groups, lanes):
    def over_core(x):
        return lax.ppermute(x, "dp", [(i, i ^ 1) for i in range(groups)])

    def over_tensor(x, shift):
        return lax.ppermute(x, "tensor", [(i, (i + shift) % lanes) for i in range(lanes)])

    def shards(inputs, latent, gain, w_latent, w_rope, w_up, grad_kv, grad_rope):
        tokens, lat = latent.shape
        rope = grad_rope.shape[1]
        width = inputs.shape[1] // lanes
        plan = Plan(groups, lanes, lat, rope)
        slots, blk, rb = plan.slots, plan.blk, plan.rb
        me, lane = lax.axis_index("dp"), lax.axis_index("tensor")
        ids = jnp.stack([me, lane]).astype(jnp.int32)
        gain = gain[None, :]

        def over_plane(x, slot):
            return lax.ppermute(x, "dp", [(i, i ^ plan.across(slot, i % 2)) for i in range(groups)])

        held = {0: w_up}
        for slot in slots[1:]:
            if popcount(slot) == 1:
                held[slot] = over_plane(w_up if slot == 1 else after(w_up, held[1]), slot)
        if width % 128 == 0:
            cut = call(functools.partial(cut_kernel, lanes), "cut", [shape(tokens, width)] * lanes,
                       0, 0, ids, inputs)
        else:
            pieces = [inputs[:, j * width:(j + 1) * width] for j in range(lanes)]
            cut = [pick(pieces, lax.rem(lane + k, lanes)) for k in range(lanes)]
        spread = [cut[0]] + [over_tensor(cut[k], k) for k in range(1, lanes)]

        kv = load(ids, grad_kv)
        early = [latent] + [over_tensor(latent, k) for k in range(1, lanes)]
        normed_t = call(functools.partial(prep_kernel, plan), "prep", shape(lat, tokens * lanes),
                        0, 0, ids, gain, *early)

        for slot in slots[1:]:
            if popcount(slot) == 1:
                held[slot] = after(held[slot], kv, normed_t, cut[0])
        for slot in slots[1:]:
            if popcount(slot) > 1:
                held[slot] = over_plane(held[slot ^ plan.hop(slot)], plan.hop(slot))
        others = {slot: over_core(held[slot]) for slot in plan.near}

        def norm_part(part, weight, before, *done):
            rows = [(others if core else held)[slot] for core in (0, 1) for slot in part]
            rows[0] = after(rows[0], *done)
            return heads_product(ids, kv, rows, before, lanes, weight)

        near_heads = norm_part(plan.near, W_M1, [])
        theirs, *mine = up_product(ids, after(normed_t, near_heads[0]), kv, len(slots), W_U)
        came = over_core(theirs)
        for slot in plan.last:
            held[slot] = after(held[slot], theirs, *spread[1:])
            others[slot] = over_core(held[slot])
        heads = norm_part(plan.last, W_M2, near_heads)

        sums = {slot: [mine[i], (came, i * blk)] for i, slot in enumerate(slots)}
        far = [slot for slot in slots if popcount(slot) > 1]
        heads = [heads[0]] + [over_tensor(heads[k], k) for k in range(1, lanes)]

        for slot in reversed(far):
            sums[slot ^ plan.hop(slot)].append(over_plane(add(after(sums[slot][0], heads[0]), *sums[slot][1:]), plan.hop(slot)))

        going = {slot: add(*sums[slot]) for slot in slots if popcount(slot) == 1}
        lows = [over_plane(block, slot) for slot, block in going.items()]

        message = call(
            functools.partial(pre_kernel, plan), "pre",
            shape(tokens + GAIN_ROWS + rope * tokens // lat, lat),
            0, 0, ids, latent, gain, grad_rope.T, *heads)
        messages = [message] + [over_tensor(message, k) for k in range(1, lanes)]

        size = lat // 2 + len(slots) * rb + 16
        other, own = call(
            functools.partial(latent_kernel, plan, tokens), "latent_part",
            [shape(size, width), shape(size, width, F32)],
            2 * lat * tokens * lanes * width, W_LAT, ids, *messages,
            *spread[:-1], after(spread[-1], *going.values()))

        columns = call(
            functools.partial(columns_kernel, plan, tokens), "columns", [shape(tokens, width)] * lanes,
            2 * lat * tokens * lanes * (width + lat), W_COL, ids, *messages[:-1],
            after(messages[-1], other), w_latent, w_rope.T)
        back = [columns[0]] + [over_tensor(columns[k], -k) for k in range(1, lanes)]
        if width % 128 != 0:
            back = [pick(back, lax.rem(j + lanes - lane, lanes)) for j in range(lanes)]

        other = over_core(other)
        grad_w_up = add(*sums[0], *lows)
        size = blk + rb + 8
        blocks = call(
            functools.partial(chip_kernel, plan), "chip_sum",
            [shape(size, width, F32)] + [shape(size, width)] * (len(slots) - 1), 0, 0, ids,
            after(own, grad_w_up), other)
        blocks = [blocks[0]] + [over_plane(b, slot) for b, slot in zip(blocks[1:], slots[1:])]
        grad_lat, grad_rope, grad_gain, grad_x = call(
            functools.partial(last_kernel, plan), "last",
            [shape(blk, width), shape(rb, width), shape(1, lat, F32), shape(tokens, width * lanes)],
            0, 0, ids, *back, *blocks)
        return grad_x, grad_w_up, grad_lat.T, grad_rope[:plan.rblk].T, grad_gain[0]

    return shards


def solution(mesh):
    in_specs = (
        P(("dp", "tensor"), None),
        P(("dp", "tensor"), None),
        P(),
        P("tensor", None),
        P("tensor", None),
        P("dp", "tensor"),
        P("dp", "tensor"),
        P(("dp", "tensor"), None),
    )
    out_specs = (
        P(("dp", "tensor"), None),
        P("dp", "tensor"),
        P("tensor", "dp"),
        P("tensor", "dp"),
        P(),
    )
    shards = make_shards(mesh.shape["dp"], mesh.shape["tensor"])
    return jax.shard_map(shards, mesh=mesh, in_specs=in_specs, out_specs=out_specs, check_vma=False)
```

```python
import functools

import jax
import jax.numpy as jnp
import numpy as np
from jax import lax
from jax.experimental import pallas as pl
from jax.experimental.pallas import tpu as pltpu
from jax.sharding import PartitionSpec as P

epsilon = 1e-06
W_U, W_M1, W_M2, W_COL, W_LAT = 2, 0, 16, 1, 8
LIMIT_U, LIMIT_M = 12, 12
F32 = jnp.float32
BF16 = jnp.bfloat16
VMEM = pl.BlockSpec(memory_space=pltpu.VMEM)
SMEM = pl.BlockSpec(memory_space=pltpu.SMEM)
GAIN_ROWS = 16


def dot(left, right, left_dim, right_dim):
    return lax.dot_general(
        left, right, (((left_dim,), (right_dim,)), ((), ())), preferred_element_type=F32
    )


def popcount(value):
    return bin(value).count("1")


def after(x, *done):
    return lax.optimization_barrier((x,) + done)[0]


def work(flops, moved, weight):
    return pl.CostEstimate(flops=weight * flops, bytes_accessed=weight * moved, transcendentals=0)


def call(body, name, out_shape, flops, weight, *args, scratch=(), limit=16):
    moved = sum(a.size * a.dtype.itemsize for a in args)
    return pl.pallas_call(
        body,
        in_specs=[SMEM] + [VMEM] * (len(args) - 1),
        out_specs=jax.tree.map(lambda _: VMEM, out_shape),
        out_shape=out_shape,
        scratch_shapes=scratch,
        compiler_params=pltpu.CompilerParams(vmem_limit_bytes=limit * 2**20),
        cost_estimate=work(flops, moved, weight),
        name=name,
    )(*args)


def split_rows(x, count, rows):
    at = lax.broadcasted_iota(jnp.int32, (rows, x.shape[1]), 0)
    result = jnp.zeros((rows, x.shape[1]), F32)
    for i in range(count):
        part = x.astype(BF16).astype(F32)
        result = jnp.where(at == i, part, result)
        x = x - part
    return result.astype(BF16)


class Plan:
    def __init__(self, groups, lanes, lat, rope):
        self.groups, self.lanes, self.lat, self.rope = groups, lanes, lat, rope
        self.axes = groups.bit_length() - 2
        self.slots = sorted(range(groups // 2), key=lambda slot: (popcount(slot), slot))
        middle = len(self.slots) // 2
        self.near, self.last = self.slots[:middle], self.slots[middle:]
        self.blk, self.rblk = lat // groups, rope // groups
        self.rb = max(self.rblk, 8)
        self.order = [(core, slot) for part in (self.near, self.last)
                      for core in (0, 1) for slot in part]

    def across(self, slot, core):
        bits = [self.axes - 1 - i if core else i for i in range(self.axes) if slot >> i & 1]
        return sum(2 << bit for bit in bits)

    def hop(self, slot):
        return 1 << (slot.bit_length() - 1)

    def rows_of(self, core):
        part = len(self.near) * self.blk
        first, second = core * part, (2 + core) * part
        return (first, first + part), (second, second + part)

    def pick_core(self, x, core):
        return jnp.concatenate([x[a:b] for a, b in self.rows_of(core)], axis=0)

    def place(self, me, order, block, stride):
        size, count = len(order) * stride, self.groups * block
        row = lax.broadcasted_iota(jnp.int32, (size, 1), 0)
        spot = jnp.full((size, 1), -1, jnp.int32)
        for b, (core, slot) in enumerate(order):
            rel = jnp.where(me % 2 == 0, self.across(slot, core) + core, self.across(slot, 1 - core) + core)
            start = (me ^ rel) * block
            inside = (row >= b * stride) & (row < b * stride + block)
            spot = jnp.where(inside, start + (row - b * stride), spot)
        column = lax.broadcasted_iota(jnp.int32, (size, count), 1)
        return (column == spot).astype(F32).astype(BF16)

    def place_latent(self, me):
        return self.place(me, self.order, self.blk, self.blk)

    def place_rope(self, me):
        order = [(core, slot) for core in (0, 1) for slot in self.slots]
        return self.place(me, order, self.rblk, self.rb)


def prep_kernel(plan, ids, gain, *refs):
    pieces, out_ref = refs[:-1], refs[-1]
    me, lane = ids[0], ids[1]
    tokens = pieces[0].shape[0]
    place = plan.place_latent(me)
    gain_col = jnp.sum(dot(place, split_rows(gain[...], 3, 8), 1, 1), axis=1, keepdims=True)
    for k, piece in enumerate(pieces):
        x = dot(place, piece[...], 1, 1)
        inverse = lax.rsqrt(jnp.sum(x * x, axis=0, keepdims=True) / plan.lat + epsilon)
        normed = (x * inverse * gain_col).astype(BF16)
        normed = jnp.concatenate([plan.pick_core(normed, 1), plan.pick_core(normed, 0)], axis=0)
        start = pl.multiple_of(lax.rem(lane - k + plan.lanes, plan.lanes) * tokens, tokens)
        out_ref[:, pl.ds(start, tokens)] = normed


def load_kernel(ids, x_ref, out_ref, sems):
    rows = x_ref.shape[0] // sems.shape[0]
    copies = [pltpu.make_async_copy(x_ref.at[pl.ds(i * rows, rows)], out_ref.at[pl.ds(i * rows, rows)],
                                    sems.at[i]) for i in range(sems.shape[0])]
    for copy in copies:
        copy.start()
    for copy in copies:
        copy.wait()


def load(ids, x):
    return pl.pallas_call(
        load_kernel,
        in_specs=[SMEM, pl.BlockSpec(memory_space=pltpu.HBM)],
        out_specs=VMEM,
        out_shape=pltpu.VMEM(x.shape, x.dtype),
        scratch_shapes=[pltpu.SemaphoreType.DMA((8,))],
        compiler_params=pltpu.CompilerParams(vmem_limit_bytes=2 * 2**20),
        cost_estimate=work(0, 0, 0),
        name="load",
    )(ids, x)


def up_kernel(ids, normed_ref, kv_ref, theirs_ref, *mine):
    half = theirs_ref.shape[0]
    rows = half // len(mine)
    depth = kv_ref.shape[1]
    step = min(depth, 1024)

    @pl.loop(0, depth // step)
    def _(k):
        at = pl.ds(pl.multiple_of(k * step, step), step)
        part = jnp.dot(normed_ref[...], kv_ref[:, at], preferred_element_type=F32)
        theirs_ref[:, at] = part[:half].astype(BF16)
        for i, out_ref in enumerate(mine):
            out_ref[:, at] = part[half + i * rows:half + (i + 1) * rows].astype(BF16)


def up_product(ids, normed_t, kv, count, weight):
    size, tokens = normed_t.shape
    depth = kv.shape[1]
    half = size // 2
    shapes = [half] + [half // count] * count
    return call(up_kernel, "up_product", [shape(rows, depth) for rows in shapes],
                2 * size * tokens * depth, weight, ids, normed_t, kv, limit=LIMIT_U)


def heads_kernel(count, lanes, ids, kv_ref, *refs):
    rows, before, outs, total = refs[:count], refs[count:-lanes - 1], refs[-lanes - 1:-1], refs[-1]
    depth = kv_ref.shape[1]
    step = min(depth, 1024)
    total[...] = jnp.zeros_like(total)

    @pl.loop(0, depth // step)
    def _(k):
        at = pl.ds(pl.multiple_of(k * step, step), step)
        total[...] += dot(kv_ref[:, at], jnp.concatenate([r[:, at] for r in rows], axis=0), 1, 1)

    tokens, columns = outs[0].shape[0], total.shape[1]
    for k, out_ref in enumerate(outs):
        start = pl.multiple_of(lax.rem(ids[1] + k, lanes) * tokens, tokens)
        if before:
            out_ref[:, :columns] = before[k][...]
        out_ref[:, out_ref.shape[1] - columns:] = total[pl.ds(start, tokens), :].astype(BF16)


def heads_product(ids, kv, rows, before, lanes, weight):
    tokens, depth = kv.shape
    width = sum(r.shape[0] for r in rows)
    out = shape(tokens // lanes, width + sum(b.shape[1] for b in before[:1]))
    return call(functools.partial(heads_kernel, len(rows), lanes), "heads_product", [out] * lanes,
                2 * tokens * depth * width, weight, ids, kv, *rows, *before,
                scratch=[pltpu.VMEM((tokens, width), F32)], limit=LIMIT_M)


def pre_kernel(plan, ids, latent, gain, rope_t, *refs):
    lanes = plan.lanes
    heads, out_ref = refs[:lanes], refs[lanes]
    tokens = latent.shape[0]
    place = plan.place_latent(ids[0])
    x = dot(latent[...], place, 1, 1)
    gain_row = jnp.sum(dot(split_rows(gain[...], 3, 8), place, 1, 1), axis=0, keepdims=True)
    grad_norm = sum(r[...].astype(F32) for r in heads)
    inverse = lax.rsqrt(jnp.sum(x * x, axis=1, keepdims=True) / plan.lat + epsilon)
    scaled = grad_norm * gain_row
    mean = jnp.sum(scaled * x, axis=1, keepdims=True) / plan.lat
    pre = inverse * scaled - x * (inverse * inverse * inverse) * mean
    out_ref[:tokens] = pre.astype(BF16)
    part = jnp.sum(grad_norm * x * inverse, axis=0, keepdims=True)
    part = jnp.sum(dot(split_rows(part, 3, 8), place, 1, 0), axis=0, keepdims=True)
    out_ref[tokens:tokens + GAIN_ROWS] = split_rows(part, 2, GAIN_ROWS)
    blocks = plan.lat // tokens
    rows = plan.rope // blocks
    out_ref[tokens + GAIN_ROWS:] = jnp.concatenate(
        [rope_t[i * rows:(i + 1) * rows, :] for i in range(blocks)], axis=1)


def rope_of(plan, message, tokens):
    blocks = plan.lat // tokens
    packed = message[tokens + GAIN_ROWS:]
    return jnp.concatenate(
        [packed[:, i * tokens:(i + 1) * tokens] for i in range(blocks)], axis=0)


def columns_kernel(plan, tokens, ids, *refs):
    lanes = plan.lanes
    messages, w_latent, w_rope_t, outs = refs[:lanes], refs[lanes], refs[lanes + 1], refs[lanes + 2:]
    pre = jnp.concatenate([m[:tokens] for m in messages], axis=0)
    pre = dot(pre, plan.place_latent(ids[0]), 1, 0).astype(BF16)
    rope = jnp.concatenate([rope_of(plan, m, tokens) for m in messages], axis=1)
    result = (dot(pre, w_latent[...], 1, 1) + dot(rope, w_rope_t[...], 0, 0)).astype(BF16)
    for k, out_ref in enumerate(outs):
        out_ref[...] = result[k * tokens:(k + 1) * tokens]


def gain_block(x, width):
    both = split_rows(x, 2, 8).astype(F32)
    row = jnp.concatenate([both[0:1], both[1:2]], axis=1)
    cut = row.shape[1]
    while cut > width:
        cut //= 2
    at = lax.broadcasted_iota(jnp.int32, (8, cut), 0)
    result = jnp.zeros((8, cut), F32)
    for i in range(row.shape[1] // cut):
        result = jnp.where(at == i, row[:, i * cut:(i + 1) * cut], result)
    if cut < width:
        result = jnp.concatenate([result, jnp.zeros((8, width - cut), F32)], axis=1)
    return result


def gain_of(block, lat):
    cut = 2 * lat
    while cut > block.shape[1]:
        cut //= 2
    row = jnp.concatenate([block[i:i + 1, :cut] for i in range(2 * lat // cut)], axis=1)
    return row[:, :lat] + row[:, lat:]


def latent_kernel(plan, tokens, ids, *refs):
    lanes = plan.lanes
    messages, spread, other_ref, own_ref = refs[:lanes], refs[lanes:2 * lanes], refs[-2], refs[-1]
    lane = ids[1]
    width = spread[0].shape[1]
    far = [lax.rem(lane - k + lanes, lanes) for k in range(lanes)]
    spread = jnp.concatenate([r[...] for r in spread], axis=0)
    pre = jnp.concatenate([m[:tokens] for m in messages], axis=0)
    rope_t = jnp.concatenate([rope_of(plan, m, tokens) for m in messages], axis=1)
    rope_t = dot(plan.place_rope(ids[0]), rope_t, 1, 0).astype(BF16)
    lat_rows = dot(pre, spread, 0, 0)
    rope_rows = dot(rope_t, spread, 1, 0)
    parts = [jnp.sum(m[tokens:tokens + GAIN_ROWS].astype(F32), axis=0, keepdims=True)
             for m in messages]
    total = jnp.zeros_like(parts[0])
    for j in range(lanes):
        term = parts[0]
        for k in range(1, lanes):
            term = jnp.where(far[j] == k, parts[k], term)
        total = total + term
    gain = gain_block(total, width)
    n = len(plan.slots) * plan.rb
    for core, ref in ((1, other_ref), (0, own_ref)):
        rows = jnp.concatenate(
            [plan.pick_core(lat_rows, core), rope_rows[core * n:(core + 1) * n],
             gain, jnp.zeros_like(gain)], axis=0)
        ref[...] = rows.astype(ref.dtype)


def chip_kernel(plan, ids, own, other, *outs):
    half, n = plan.lat // 2, len(plan.slots) * plan.rb
    width = own.shape[1]
    mine, came = own[...], other[...].astype(F32)
    total = mine + came
    gain = gain_of(mine[half + n:half + n + 8], plan.lat) + gain_of(came[half + n:half + n + 8], plan.lat)
    gain = gain_block(gain, width)
    for i, out_ref in enumerate(outs):
        rows = jnp.concatenate(
            [total[i * plan.blk:(i + 1) * plan.blk],
             total[half + i * plan.rb:half + (i + 1) * plan.rb], gain], axis=0)
        out_ref[...] = rows.astype(out_ref.dtype)


def last_kernel(plan, ids, *refs):
    count = len(plan.slots)
    back, sums = refs[:plan.lanes], refs[plan.lanes:plan.lanes + count]
    lat_ref, rope_ref, gain_ref, x_ref = refs[plan.lanes + count:]
    width = back[0].shape[1]
    for k, piece in enumerate(back):
        if width % 128 == 0:
            start = pl.multiple_of(lax.rem(ids[1] + k, plan.lanes) * width, width)
        else:
            start = k * width
        x_ref[:, pl.ds(start, width)] = piece[...]
    blk, rb = plan.blk, plan.rb
    me = ids[0]
    sums = [r[...].astype(F32) for r in sums]
    total = sum(s[:blk + rb] for s in sums)
    lat_ref[...] = total[:blk].astype(BF16)
    rope_ref[...] = total[blk:blk + rb].astype(BF16)
    parts = [gain_of(s[blk + rb:blk + rb + 8], plan.lat) for s in sums]
    gain = jnp.zeros_like(parts[0])
    for chip in range(plan.groups // 2):
        term = jnp.zeros_like(parts[0])
        for slot, part in zip(plan.slots, parts):
            rel = jnp.where(me % 2 == 0, plan.across(slot, 0) // 2, plan.across(slot, 1) // 2)
            term = jnp.where((rel ^ (me // 2)) == chip, part, term)
        gain = gain + term
    gain_ref[...] = gain


def cut_kernel(lanes, ids, x, *outs):
    width = outs[0].shape[1]
    for k, out_ref in enumerate(outs):
        start = pl.multiple_of(lax.rem(ids[1] + k, lanes) * width, width)
        out_ref[...] = x[:, pl.ds(start, width)]


def pick(pieces, index):
    result = pieces[0]
    for i in range(1, len(pieces)):
        result = jnp.where(index == i, pieces[i], result)
    return result


def add_kernel(*refs):
    refs[-1][...] = sum(r[...].astype(F32) for r in refs[:-1]).astype(BF16)


def add(*parts):
    parts = [p if isinstance(p, tuple) else (p, 0) for p in parts]
    rows, depth = parts[0][0].shape
    step = min(depth, 2048)
    return pl.pallas_call(
        add_kernel,
        grid=(depth // step,),
        in_specs=[pl.BlockSpec((rows, step), lambda k, at=at: (at // rows, k)) for _, at in parts],
        out_specs=pl.BlockSpec((rows, step), lambda k: (0, k)),
        out_shape=shape(rows, depth),
        compiler_params=pltpu.CompilerParams(vmem_limit_bytes=8 * 2**20),
        cost_estimate=work(0, 2 * rows * depth * (len(parts) + 1), 1),
        name="add",
    )(*[p for p, _ in parts])


def shape(rows, columns, dtype=BF16):
    return jax.ShapeDtypeStruct((rows, columns), dtype)


def make_shards(groups, lanes):
    def over_core(x):
        return lax.ppermute(x, "dp", [(i, i ^ 1) for i in range(groups)])

    def over_tensor(x, shift):
        return lax.ppermute(x, "tensor", [(i, (i + shift) % lanes) for i in range(lanes)])

    def shards(inputs, latent, gain, w_latent, w_rope, w_up, grad_kv, grad_rope):
        tokens, lat = latent.shape
        rope = grad_rope.shape[1]
        width = inputs.shape[1] // lanes
        plan = Plan(groups, lanes, lat, rope)
        slots, blk, rb = plan.slots, plan.blk, plan.rb
        me, lane = lax.axis_index("dp"), lax.axis_index("tensor")
        ids = jnp.stack([me, lane]).astype(jnp.int32)
        gain = gain[None, :]

        def over_plane(x, slot):
            return lax.ppermute(x, "dp", [(i, i ^ plan.across(slot, i % 2)) for i in range(groups)])

        held = {0: w_up}
        for slot in slots[1:]:
            if popcount(slot) == 1:
                held[slot] = over_plane(w_up if slot == 1 else after(w_up, held[1]), slot)
        if width % 128 == 0:
            cut = call(functools.partial(cut_kernel, lanes), "cut", [shape(tokens, width)] * lanes,
                       0, 0, ids, inputs)
        else:
            pieces = [inputs[:, j * width:(j + 1) * width] for j in range(lanes)]
            cut = [pick(pieces, lax.rem(lane + k, lanes)) for k in range(lanes)]
        spread = [cut[0]] + [over_tensor(cut[k], k) for k in range(1, lanes)]

        kv = load(ids, grad_kv)
        early = [latent] + [over_tensor(latent, k) for k in range(1, lanes)]
        normed_t = call(functools.partial(prep_kernel, plan), "prep", shape(lat, tokens * lanes),
                        0, 0, ids, gain, *early)

        for slot in slots[1:]:
            if popcount(slot) == 1:
                held[slot] = after(held[slot], kv, cut[0], *early[1:])
        for slot in slots[1:]:
            if popcount(slot) > 1:
                held[slot] = over_plane(held[slot ^ plan.hop(slot)], plan.hop(slot))
        others = {slot: over_core(held[slot]) for slot in plan.near}

        def norm_part(part, weight, before, *done):
            rows = [(others if core else held)[slot] for core in (0, 1) for slot in part]
            rows[0] = after(rows[0], *done)
            return heads_product(ids, kv, rows, before, lanes, weight)

        near_heads = norm_part(plan.near, W_M1, [])
        theirs, *mine = up_product(ids, after(normed_t, near_heads[0]), kv, len(slots), W_U)
        came = over_core(theirs)
        for slot in plan.last:
            held[slot] = after(held[slot], theirs, spread[1], spread[-1])
            others[slot] = over_core(held[slot])
        heads = norm_part(plan.last, W_M2, near_heads)

        sums = {slot: [mine[i], (came, i * blk)] for i, slot in enumerate(slots)}
        far = [slot for slot in slots if popcount(slot) > 1]
        heads = [heads[0]] + [over_tensor(heads[k], k) for k in range(1, lanes)]

        for slot in reversed(far):
            sums[slot ^ plan.hop(slot)].append(over_plane(add(after(sums[slot][0], *heads[1:], *spread[2:-1]), *sums[slot][1:]), plan.hop(slot)))

        going = {slot: add(*sums[slot]) for slot in slots if popcount(slot) == 1}
        lows = [over_plane(block, slot) for slot, block in going.items()]

        message = call(
            functools.partial(pre_kernel, plan), "pre",
            shape(tokens + GAIN_ROWS + rope * tokens // lat, lat),
            0, 0, ids, latent, gain, grad_rope.T, *heads)
        messages = [message] + [over_tensor(message, k) for k in range(1, lanes)]

        size = lat // 2 + len(slots) * rb + 16
        other, own = call(
            functools.partial(latent_kernel, plan, tokens), "latent_part",
            [shape(size, width), shape(size, width, F32)],
            2 * lat * tokens * lanes * width, W_LAT, ids, *messages, *spread)

        columns = call(
            functools.partial(columns_kernel, plan, tokens), "columns", [shape(tokens, width)] * lanes,
            2 * lat * tokens * lanes * (width + lat), W_COL, ids, *messages[:-1],
            after(messages[-1], other), w_latent, w_rope.T)
        back = [columns[0]] + [over_tensor(columns[k], -k) for k in range(1, lanes)]
        if width % 128 != 0:
            back = [pick(back, lax.rem(j + lanes - lane, lanes)) for j in range(lanes)]

        other = over_core(other)
        grad_w_up = add(*sums[0], *lows)
        size = blk + rb + 8
        blocks = call(
            functools.partial(chip_kernel, plan), "chip_sum",
            [shape(size, width, F32)] + [shape(size, width)] * (len(slots) - 1), 0, 0, ids,
            after(own, grad_w_up), other)
        blocks = [blocks[0]] + [over_plane(b, slot) for b, slot in zip(blocks[1:], slots[1:])]
        grad_lat, grad_rope, grad_gain, grad_x = call(
            functools.partial(last_kernel, plan), "last",
            [shape(blk, width), shape(rb, width), shape(1, lat, F32), shape(tokens, width * lanes)],
            0, 0, ids, *back, *blocks)
        return grad_x, grad_w_up, grad_lat.T, grad_rope[:plan.rblk].T, grad_gain[0]

    return shards


def solution(mesh):
    in_specs = (
        P(("dp", "tensor"), None),
        P(("dp", "tensor"), None),
        P(),
        P("tensor", None),
        P("tensor", None),
        P("dp", "tensor"),
        P("dp", "tensor"),
        P(("dp", "tensor"), None),
    )
    out_specs = (
        P(("dp", "tensor"), None),
        P("dp", "tensor"),
        P("tensor", "dp"),
        P("tensor", "dp"),
        P(),
    )
    shards = make_shards(mesh.shape["dp"], mesh.shape["tensor"])
    return jax.shard_map(shards, mesh=mesh, in_specs=in_specs, out_specs=out_specs, check_vma=False)
```
